32 devices in a mesh: group: 2 (over x), row: 16 (over z, y, core).
Axes of the slice: x: 2, y: 2, z: 4, core: 2. Of those that a mesh axis runs over, the one named last changes fastest.
Arguments:
- anc_cov: bfloat16 [8192, 4096], P(('group', 'row')), parts along dimension 0, as said below
- mid_factor: bfloat16 [8192, 1024], P(('group', 'row')), parts along dimension 0, may hold values from -0.125 to 0.125
- mid_diag_inv: bfloat16 [2048, 1024], P(('group', 'row')), parts along dimension 0, as said below
- leaf_factor: bfloat16 [10240, 512], P(('group', 'row')), parts along dimension 0, may hold values from -0.125 to 0.125
- leaf_diag_inv: bfloat16 [2048, 512], P(('group', 'row')), parts along dimension 0, as said below
- leaf_rows: int32 [2, 80], replicated, may hold values from 0 to 159, as said below
Outputs:
- mid_block: float32 [2048, 1024], P(('group', 'row')), parts along dimension 0
- leaf_block: float32 [2048, 512], P(('group', 'row')), parts along dimension 0
The draws below stay inside these ranges and needn't reach their ends.
There are 2 independent parts, one for each index of `group`. The reference program is written for one: setup_inputs(seed, part) draws one part's arguments, and reference() takes and returns one part's arrays. A program takes and returns all parts, laid end to end along the dimension named above; an argument that names none is the same for every part. Nothing has to cross between parts.
Inputs may be any that keep to these rules, and one draw needn't show every extreme that they name: `leaf_rows`: each row lists 80 distinct block numbers in increasing order; every row holds the first and the last block. `anc_cov`: symmetric in every draw. `mid_diag_inv`: symmetric in every draw. `leaf_diag_inv`: each of the two stacked 512 x 512 blocks is symmetric in every draw.
All inputs are finite; a program needn't handle non-finite values.
Results may differ from the reference program's by a relative error of at most 0.0003.
Values may be sent and summed in bfloat16 or wider, within the bound.
No kernel may reach another device: no remote copies, remote signals or barrier semaphores. Data moves between devices by JAX's collectives and lax.ppermute only.
A program may use at most 128 MiB of HBM per device.

```python
import math
import jax
import jax.numpy as jnp
from jax import lax

ANC = 4096
MID = 1024
LEAF = 512
TILE = 32
KEEP = 80


def spd_block(key, order, low, high, spread):
    key_scale, key_noise = jax.random.split(key)
    scales = jnp.exp(jax.random.uniform(key_scale, (order,), jnp.float32, math.log(low), math.log(high)))
    noise = jax.random.uniform(key_noise, (order, order), jnp.float32, -spread, spread) / math.sqrt(order)
    symmetric = 0.5 * (noise + noise.T)
    identity = jnp.eye(order, dtype=jnp.float32)
    rooted = jnp.sqrt(scales)
    return rooted[:, None] * (identity + symmetric) * rooted[None, :]


def draw_anc_cov(key, part):
    key = jax.random.fold_in(key, 11)
    return spd_block(key, ANC, 0.5, 2.0, 0.6).astype(jnp.bfloat16)


def draw_mid_diag_inv(key, part):
    key = jax.random.fold_in(key, 23)
    return spd_block(key, MID, 0.5, 2.0, 0.6).astype(jnp.bfloat16)


def draw_leaf_diag_inv(key, part):
    key = jax.random.fold_in(key, 37)
    first = spd_block(jax.random.fold_in(key, 1), LEAF, 0.5, 2.0, 0.6)
    second = spd_block(jax.random.fold_in(key, 2), LEAF, 0.5, 2.0, 0.6)
    return jnp.concatenate([first, second], axis=0).astype(jnp.bfloat16)


def draw_leaf_rows(key, part):
    key = jax.random.fold_in(key, 41)
    inner = (MID + ANC) // TILE
    listed = []
    for child in range(2):
        shuffled = jax.random.permutation(jax.random.fold_in(key, child), inner - 2) + 1
        chosen = jnp.concatenate([jnp.zeros((1,), jnp.int32), shuffled[:KEEP - 2].astype(jnp.int32), jnp.full((1,), inner - 1, jnp.int32)])
        listed.append(jnp.sort(chosen))
    return jnp.stack(listed).astype(jnp.int32)


def block_scale(rng, dims, cuts, smallest, high):
    loudness, own = 1.0, jax.random.fold_in(rng, 6)
    for dim, blocks in cuts:
        draws = jnp.exp(jax.random.uniform(jax.random.fold_in(own, dim), (blocks,), jnp.float32, smallest / len(cuts), high / len(cuts)))
        loudness = loudness * jnp.repeat(draws, dims[dim] // blocks).reshape([-1 if axis == dim else 1 for axis in range(len(dims))])
    return loudness


def centred(own_key, shape, scale, reach, pieces=(), kind=jnp.bfloat16):
    entries = jax.random.normal(own_key, shape, jnp.float32) * scale
    if len(pieces) > 0:
        entries = block_scale(own_key, shape, pieces, -0.22, 0.18) * entries
    return jnp.clip(entries, min=-reach, max=reach).astype(kind)


def setup_inputs(seed: int = 0, part: int = 0) -> dict:
    streams_of = jax.random.split(jax.random.key(seed), 7)
    own_keys = jax.random.split(jax.random.fold_in(streams_of[6], part), 7)
    anc_cov = draw_anc_cov(jax.random.fold_in(jax.random.fold_in(streams_of[6], part), 71), part)
    mid_factor = centred(own_keys[1], (ANC, MID), (ANC // 2) ** -0.5, 0.125, ((0, 16),))
    mid_diag_inv = draw_mid_diag_inv(jax.random.fold_in(jax.random.fold_in(streams_of[6], part), 71), part)
    leaf_factor = centred(own_keys[3], (2 * KEEP * TILE, LEAF), (KEEP * TILE) ** -0.5, 0.125, ((0, 16),))
    leaf_diag_inv = draw_leaf_diag_inv(jax.random.fold_in(jax.random.fold_in(streams_of[6], part), 71), part)
    leaf_rows = draw_leaf_rows(jax.random.fold_in(streams_of[6], 71), part)
    return {"anc_cov": anc_cov, "mid_factor": mid_factor, "mid_diag_inv": mid_diag_inv, "leaf_factor": leaf_factor, "leaf_diag_inv": leaf_diag_inv, "leaf_rows": leaf_rows}


def across(left, right):
    return lax.dot_general(left.astype(jnp.float32), right.astype(jnp.float32), (((0,), (0,)), ((), ())), precision=lax.Precision.HIGHEST, preferred_element_type=jnp.float32)


def exact_dot(left, right):
    return jnp.dot(left.astype(jnp.float32), right.astype(jnp.float32), precision=lax.Precision.HIGHEST, preferred_element_type=jnp.float32)


def embed_factor(block_list, factor, tiles_total):
    listed = block_list.shape[0]
    tiled = factor.reshape(listed, -1)
    matches = block_list[None, :] == jnp.arange(tiles_total, dtype=jnp.int32)[:, None]
    position = jnp.sum(jnp.where(matches, jnp.arange(listed, dtype=jnp.int32)[None, :], 0), axis=1).astype(jnp.int32)
    present = jnp.any(matches, axis=1)
    picked = jnp.take(tiled, position, axis=0)
    picked = jnp.where(present[:, None], picked, jnp.zeros_like(picked))
    return picked.reshape(tiles_total * (factor.shape[0] // listed), factor.shape[1])


def embed_both(leaf_rows, leaf_factor, tiles_total):
    halfway = leaf_factor.shape[0] // 2
    first = embed_factor(leaf_rows[0], leaf_factor[:halfway], tiles_total)
    second = embed_factor(leaf_rows[1], leaf_factor[halfway:], tiles_total)
    return jnp.concatenate([first, second], axis=1)


def reference(anc_cov, mid_factor, mid_diag_inv, leaf_factor, leaf_diag_inv, leaf_rows):
    product = jnp.dot(anc_cov, mid_factor, preferred_element_type=jnp.float32)
    cross = -product
    mid_block = mid_diag_inv.astype(jnp.float32) - across(mid_factor, cross)
    tiles_total = (MID + ANC) // TILE
    embedded = embed_both(leaf_rows, leaf_factor, tiles_total)
    embed_mid = embedded[:MID]
    embed_anc = embedded[MID:]
    spread_low = exact_dot(cross, embed_mid) + jnp.dot(anc_cov, embed_anc, preferred_element_type=jnp.float32)
    mid_image = jnp.dot(mid_diag_inv, embed_mid, preferred_element_type=jnp.float32) - across(mid_factor, spread_low)
    image = jnp.concatenate([mid_image, spread_low], axis=0)
    first = across(embedded[:, :LEAF], image[:, :LEAF])
    second = across(embedded[:, LEAF:], image[:, LEAF:])
    leaf_block = leaf_diag_inv.astype(jnp.float32) + jnp.concatenate([first, second], axis=0)
    return mid_block, leaf_block
```

```python
import jax
import jax.numpy as jnp
from jax import lax
from jax.experimental import pallas as pl
from jax.experimental.pallas import tpu as pltpu
from jax.sharding import PartitionSpec as P

TILE = 32
F32 = jnp.float32
BF16 = jnp.bfloat16


def ring_order(chips, parts):
    if parts == 2 and chips % 2 == 0:
        return list(range(0, chips, 2)) + list(range(chips - 1, 0, -2))
    return list(range(chips))


def split(x):
    high = x.astype(BF16)
    return high, (x - high.astype(F32)).astype(BF16)


def mm(a, b):
    return lax.dot_general(a, b, (((1,), (0,)), ((), ())), preferred_element_type=F32)


def mmt(a, b):
    return lax.dot_general(a, b, (((0,), (0,)), ((), ())), preferred_element_type=F32)


def place_of(chip, chips, snake):
    return jnp.where(chip % 2 == 0, chip // 2, chips - 1 - chip // 2) if snake else chip


def chip_at(place, chips, snake):
    place = lax.rem(place, chips)
    return jnp.where(2 * place < chips, 2 * place, 2 * (chips - 1 - place) + 1) if snake else place


def mid_kernel(chips, snake, *refs):
    half = chips // 2
    device_ref, a_refs, f_refs = refs[0], refs[1:3], refs[3 : 3 + 2 * (half + 1)]
    high_ref, low_ref = refs[5 + 2 * half : 7 + 2 * half]
    y_refs = refs[7 + 2 * half : 7 + 2 * half + chips]
    left, right, turned, picked, stacked, sems = refs[7 + 2 * half + chips :]
    device = device_ref[0]
    chip, core = device // 2, device % 2
    place = place_of(chip, chips, snake)
    rows = f_refs[0].shape[0]
    mid = f_refs[0].shape[1]
    copies = []
    for step in range(half + 1):
        owner = chip_at(place + step, chips, snake)
        for side in range(2):
            lane = pl.multiple_of((2 * owner + (core if side == 0 else 1 - core)) * rows, rows)
            at = (2 * step + side) * rows
            for k in range(2):
                source, target = a_refs[k].at[:, pl.ds(lane, rows)], left.at[k * rows : (k + 1) * rows, at : at + rows]
                copies.append(pltpu.make_async_copy(source, target, sems.at[len(copies)]))
            source, target = f_refs[2 * step + side], right.at[at : at + rows, :]
            copies.append(pltpu.make_async_copy(source, target, sems.at[len(copies)]))
    for copy in copies:
        copy.start()
    for copy in copies[:6]:
        copy.wait()
    near = 2 * rows
    left[:, :near] = left[:, :near] * jnp.bfloat16(0.5)
    far = near + 2 * rows * (half // 2)
    for copy in copies[6 : 6 * (1 + half // 2)]:
        copy.wait()
    cross = mm(left[:, :far], right[:far, :])
    for copy in copies[6 * (1 + half // 2) :]:
        copy.wait()
    high, low = split(cross + mm(left[:, far:], right[far:, :]))
    high_ref[...] = high
    low_ref[...] = low
    factor = right[: 2 * rows, :]
    for k, x in enumerate((factor, high, low)):
        turned[k * mid : (k + 1) * mid, :] = x.T
    stacked[: 2 * rows, :] = high
    stacked[2 * rows : 4 * rows, :] = low
    stacked[4 * rows : 6 * rows, :] = factor
    stacked[6 * rows :, :] = factor
    strip = mid // (2 * chips)
    for s in range(chips):
        first = pl.multiple_of((2 * chip_at(place + s, chips, snake) + core) * strip, strip)
        for k, which in enumerate((0, 0, 1, 2)):
            picked[s * strip : (s + 1) * strip, k * 2 * rows : (k + 1) * 2 * rows] = turned[
                pl.ds(which * mid + first, strip), :
            ]
    y = mm(picked[...], stacked[...])
    for s in range(chips):
        y_refs[s][...] = y[s * strip : (s + 1) * strip, :]


def leaf_kernel(chips, snake, *refs):
    half = chips // 2
    device_ref, list_ref, a_refs, f_refs, d_refs = refs[0], refs[1], refs[2:4], refs[4:6], refs[6:8]
    high_ref, low_ref = refs[8:10]
    parts = refs[10 : 10 + 2 * chips]
    keep_refs = refs[10 + 2 * chips : 10 + 3 * chips]
    give_ref, wide, left, right, factors, diags, highs, lows, result, sems, embed_sem = refs[10 + 3 * chips :]
    device = device_ref[0]
    chip, core = device // 2, device % 2
    place = place_of(chip, chips, snake)
    rows, mid = f_refs[0].shape
    leaf = wide.shape[1]
    count = parts[0].shape[0] // TILE
    chip_rows = 2 * rows
    strip = d_refs[0].shape[0]
    copies = []

    def fetch(source, target):
        copies.append(pltpu.make_async_copy(source, target, sems.at[len(copies)]))
        copies[-1].start()

    for k in range(2):
        fetch(f_refs[k], factors.at[k * rows : (k + 1) * rows, :])
        fetch(d_refs[k], diags.at[k * strip : (k + 1) * strip, :])
    fetch(high_ref, highs)
    fetch(low_ref, lows)
    early = len(copies)
    for step in range(half + 1):
        lane = pl.multiple_of(chip_at(place + step, chips, snake) * chip_rows, chip_rows)
        at = step * chip_rows
        for k in range(2):
            fetch(a_refs[k].at[:, pl.ds(lane, chip_rows)], left.at[k * rows : (k + 1) * rows, at : at + chip_rows])
    wide[...] = jnp.zeros_like(wide)
    for slot in range(chips):
        source = chip_at(place + chips - slot, chips, snake)

        @pl.when(source // half == core)
        def _():
            for side in range(2):
                first = (2 * (source % half) + (core if side == 0 else 1 - core)) * count
                for i in range(count):
                    to = pl.multiple_of(list_ref[core, first + i] * TILE, TILE)
                    block = parts[2 * slot + side].at[i * TILE : (i + 1) * TILE, :]
                    pltpu.make_async_copy(block, wide.at[pl.ds(to, TILE), :], embed_sem).start()

    every = wide.at[: chips * count * TILE, :]
    pltpu.make_async_copy(every, every, embed_sem).wait()
    for step in range(half + 1):
        owner = chip_at(place + step, chips, snake)
        lane = pl.multiple_of(owner * chip_rows, chip_rows)
        at = step * chip_rows
        right[at : at + chip_rows, :] = wide[pl.ds(pl.multiple_of(mid + lane, chip_rows), chip_rows), :]
    at = half * chip_rows
    right[at:, :] = jnp.where(place < half, right[at:, :], jnp.zeros_like(right[at:, :]))
    for copy in copies[:early]:
        copy.wait()
    embed_mid = wide[:mid, :]
    other = 2 * chip + 1 - core
    own = jnp.concatenate(
        [wide[pl.ds(pl.multiple_of(mid + d * rows, rows), rows), :].astype(F32) for d in (device, other)]
    )
    g_high, g_low = split(own - mm(factors[...], embed_mid))
    spread = mm(highs[...], embed_mid) + mm(lows[...], embed_mid)
    i_high, i_low = split(mm(diags[...], embed_mid))
    for copy in copies[early:]:
        copy.wait()
    left[:, :chip_rows] = left[:, :chip_rows] * jnp.bfloat16(0.5)
    s_high, s_low = split(mm(left[...], right[...]) - spread)
    inner = mmt(g_high, s_high) + mmt(g_high, s_low) + mmt(g_low, s_high)
    total = inner + inner.T
    own_mid = jnp.concatenate(
        [wide[pl.ds(pl.multiple_of(d * strip, strip), strip), :] for d in (device, other)]
    )
    result[...] = total + mmt(own_mid, i_high) + mmt(own_mid, i_low)
    band = leaf // chips
    for s in range(chips):
        target = chip_at(place + s, chips, snake)
        mine = target // half == core
        for ref, side in ((keep_refs[s], core), (give_ref.at[s * band : (s + 1) * band, :], 1 - core)):
            value = result[pl.ds(pl.multiple_of((2 * (target % half) + side) * band, band), band), :]
            ref[...] = jnp.where(mine, value, jnp.zeros_like(value))


def solution(mesh):
    parts, devices = mesh.shape["group"], mesh.shape["row"]
    chips = devices // 2
    half = chips // 2
    snake = parts == 2
    order = ring_order(chips, parts)

    def perm(step, keep=lambda source, target, core: True):
        pairs = []
        for p in range(chips):
            target = (p + step) % chips
            for core in range(2):
                if keep(p, target, core):
                    pairs.append((order[p] * 2 + core, order[target] * 2 + core))
        return pairs

    def child_of(p):
        return order[p % chips] // half

    swap_pairs = [(d, d ^ 1) for d in range(devices)]

    def swap(x):
        return lax.ppermute(x, "row", swap_pairs)

    def ring_sum(terms):
        far = terms[half]
        cut = far.shape[0] // 2
        up = lax.ppermute(far[:cut], "row", perm(1))
        down = lax.ppermute(far[cut:], "row", perm(-1))
        up = terms[half - 1] + jnp.pad(up, ((0, cut), (0, 0)))
        down = terms[half + 1] + jnp.pad(down, ((cut, 0), (0, 0)))
        for s in range(half - 1, 0, -1):
            up = lax.ppermute(up, "row", perm(1))
            down = lax.ppermute(down, "row", perm(-1))
            if s > 1:
                up = up + terms[s - 1]
                down = down + terms[chips - s + 1]
        return terms[0] + up + down

    vmem = pl.BlockSpec(memory_space=pltpu.VMEM)
    smem = pl.BlockSpec(memory_space=pltpu.SMEM)
    anywhere = pl.BlockSpec(memory_space=pl.ANY)
    mid_params = pltpu.CompilerParams(vmem_limit_bytes=32 * 2**20)
    leaf_params = pltpu.CompilerParams(vmem_limit_bytes=28 * 2**20)

    def local(anc_cov, mid_factor, mid_diag_inv, leaf_factor, leaf_diag_inv, leaf_rows):
        device = lax.axis_index("row")
        device_word = device.astype(jnp.int32).reshape(1)
        rows, anc = anc_cov.shape
        mid = mid_factor.shape[1]
        leaf = leaf_factor.shape[1]

        leaf_flow = leaf_factor
        leaf_parts = [leaf_factor, swap(leaf_factor)]
        flow = mid_factor
        factors = [mid_factor, swap(mid_factor)]
        anc_swapped = swap(anc_cov)
        diag_swapped = swap(mid_diag_inv)
        done = 0
        for step in range(1, chips):
            due = min(half, (step * half - 1) // (chips - 1))
            while done < due:
                done += 1
                pairs = perm(-1, (lambda s, t, c: t < half) if done == half else (lambda s, t, c: True))
                flow = lax.ppermute(flow, "row", pairs)
                factors += [flow, swap(flow)]
                flow, leaf_flow = lax.optimization_barrier((flow, leaf_flow))
            leaf_flow = lax.ppermute(leaf_flow, "row", perm(1))
            leaf_parts += [leaf_flow, swap(leaf_flow)]
        while done < half:
            done += 1
            pairs = perm(-1, (lambda s, t, c: t < half) if done == half else (lambda s, t, c: True))
            flow = lax.ppermute(flow, "row", pairs)
            factors += [flow, swap(flow)]

        strip = mid // devices
        depth = 2 * rows * (half + 1)
        outs = pl.pallas_call(
            lambda *refs: mid_kernel(chips, snake, *refs),
            out_shape=[jax.ShapeDtypeStruct((2 * rows, mid), BF16)] * 2
            + [jax.ShapeDtypeStruct((strip, mid), F32)] * chips,
            in_specs=[smem] + [anywhere] * (2 + len(factors)),
            out_specs=[vmem] * (2 + chips),
            scratch_shapes=[
                pltpu.VMEM((2 * rows, depth), BF16),
                pltpu.VMEM((depth, mid), BF16),
                pltpu.VMEM((3 * mid, 2 * rows), BF16),
                pltpu.VMEM((mid // 2, 8 * rows), BF16),
                pltpu.VMEM((8 * rows, mid), BF16),
                pltpu.SemaphoreType.DMA((6 * (half + 1),)),
            ],
            compiler_params=mid_params,
            cost_estimate=pl.CostEstimate(flops=15 * 10**9, bytes_accessed=14 * 2**20, transcendentals=0),
            name="mid_blocks",
        )(device_word, anc_cov, anc_swapped, *factors)
        c_high, c_low, mid_terms = outs[0], outs[1], outs[2:]
        mid_block = mid_diag_inv.astype(F32) + ring_sum(mid_terms)

        band = leaf // chips
        *keep, give = pl.pallas_call(
            lambda *refs: leaf_kernel(chips, snake, *refs),
            out_shape=[jax.ShapeDtypeStruct((band, leaf), F32)] * chips + [jax.ShapeDtypeStruct((leaf, leaf), F32)],
            in_specs=[smem, smem] + [anywhere] * (8 + 2 * chips),
            out_specs=[vmem] * (chips + 1),
            scratch_shapes=[
                pltpu.VMEM((mid + anc, leaf), BF16),
                pltpu.VMEM((2 * rows, depth), BF16),
                pltpu.VMEM((depth, leaf), BF16),
                pltpu.VMEM((2 * rows, mid), BF16),
                pltpu.VMEM((2 * strip, mid), BF16),
                pltpu.VMEM((2 * rows, mid), BF16),
                pltpu.VMEM((2 * rows, mid), BF16),
                pltpu.VMEM((leaf, leaf), F32),
                pltpu.SemaphoreType.DMA((6 + 2 * (half + 1),)),
                pltpu.SemaphoreType.DMA,
            ],
            compiler_params=leaf_params,
            cost_estimate=pl.CostEstimate(flops=2 * 10**10, bytes_accessed=20 * 2**20, transcendentals=0),
            name="leaf_blocks",
        )(
            device_word, leaf_rows, anc_cov, anc_swapped, factors[0], factors[1], mid_diag_inv, diag_swapped,
            c_high, c_low, *leaf_parts,
        )
        got = swap(give)
        leaf_terms = [keep[s] + got[s * band : (s + 1) * band] for s in range(chips)]
        leaf_block = leaf_diag_inv.astype(F32) + ring_sum(leaf_terms)
        return mid_block, leaf_block

    placed = (
        P(("group", "row"), None),
        P(("group", "row"), None),
        P(("group", "row"), None),
        P(("group", "row"), None),
        P(("group", "row"), None),
        P(),
    )
    return jax.shard_map(
        local,
        mesh=mesh,
        in_specs=placed,
        out_specs=(P(("group", "row"), None), P(("group", "row"), None)),
        check_vma=False,
    )
```

```python
import jax
import jax.numpy as jnp
from jax import lax
from jax.experimental import pallas as pl
from jax.experimental.pallas import tpu as pltpu
from jax.sharding import PartitionSpec as P

TILE = 32
F32 = jnp.float32
BF16 = jnp.bfloat16


def ring_order(chips, parts):
    if parts == 2 and chips % 2 == 0:
        return list(range(0, chips, 2)) + list(range(chips - 1, 0, -2))
    return list(range(chips))


def split(x):
    high = x.astype(BF16)
    return high, (x - high.astype(F32)).astype(BF16)


def mm(a, b):
    return lax.dot_general(a, b, (((1,), (0,)), ((), ())), preferred_element_type=F32)


def mmt(a, b):
    return lax.dot_general(a, b, (((0,), (0,)), ((), ())), preferred_element_type=F32)


def place_of(chip, chips, snake):
    return jnp.where(chip % 2 == 0, chip // 2, chips - 1 - chip // 2) if snake else chip


def chip_at(place, chips, snake):
    place = lax.rem(place, chips)
    return jnp.where(2 * place < chips, 2 * place, 2 * (chips - 1 - place) + 1) if snake else place


def fetch(copies, source, target, sems):
    copies.append(pltpu.make_async_copy(source, target, sems.at[len(copies)]))
    copies[-1].start()


def fetch_columns(copies, a_refs, first, rows, target, at, sems):
    lane = pl.multiple_of(first, rows)
    for k in range(2):
        into = target.at[k * rows : (k + 1) * rows, at : at + rows]
        fetch(copies, a_refs[k].at[:, pl.ds(lane, rows)], into, sems)


def near_kernel(chips, snake, *refs):
    half = chips // 2
    device_ref, a_refs, f_refs = refs[0], refs[1:3], refs[3 : 3 + 2 * half]
    cross_ref, left, right, sems = refs[3 + 2 * half :]
    device = device_ref[0]
    chip, core = device // 2, device % 2
    place = place_of(chip, chips, snake)
    rows = f_refs[0].shape[0]
    copies = []
    for step in range(half):
        owner = chip_at(place + step, chips, snake)
        for side in range(2):
            at = (2 * step + side) * rows
            fetch_columns(copies, a_refs, (2 * owner + (core if side == 0 else 1 - core)) * rows, rows, left, at, sems)
            fetch(copies, f_refs[2 * step + side], right.at[at : at + rows, :], sems)
    for copy in copies[:6]:
        copy.wait()
    left[:, : 2 * rows] = left[:, : 2 * rows] * jnp.bfloat16(0.5)
    cut = 2 * rows * (half // 2)
    for copy in copies[6 : 6 * (half // 2)]:
        copy.wait()
    cross = mm(left[:, :cut], right[:cut, :])
    for copy in copies[6 * (half // 2) :]:
        copy.wait()
    cross_ref[...] = cross + mm(left[:, cut:], right[cut:, :])


def mid_kernel(chips, snake, *refs):
    half = chips // 2
    device_ref, a_refs, own_refs, far_refs, cross_ref = refs[0], refs[1:3], refs[3:5], refs[5:7], refs[7]
    high_ref, low_ref = refs[8:10]
    y_refs, up_ref, down_ref = refs[10 : 10 + chips], refs[10 + chips], refs[11 + chips]
    left, right, own, cross, turned, picked, stacked, sems = refs[12 + chips :]
    device = device_ref[0]
    chip, core = device // 2, device % 2
    place = place_of(chip, chips, snake)
    rows, mid = own_refs[0].shape
    copies = []
    fetch(copies, cross_ref, cross, sems)
    for side in range(2):
        fetch(copies, own_refs[side], own.at[side * rows : (side + 1) * rows, :], sems)
    owner = chip_at(place + half, chips, snake)
    for side in range(2):
        lane = (2 * owner + (core if side == 0 else 1 - core)) * rows
        fetch_columns(copies, a_refs, lane, rows, left, side * rows, sems)
        fetch(copies, far_refs[side], right.at[side * rows : (side + 1) * rows, :], sems)
    for copy in copies:
        copy.wait()
    factor = own[...]
    high, low = split(cross[...] + mm(left[...], right[...]))
    high_ref[...] = high
    low_ref[...] = low
    for k, x in enumerate((factor, high, low)):
        turned[k * mid : (k + 1) * mid, :] = x.T
    stacked[: 2 * rows, :] = high
    stacked[2 * rows : 4 * rows, :] = low
    stacked[4 * rows : 6 * rows, :] = factor
    stacked[6 * rows :, :] = factor
    strip = mid // (2 * chips)
    for s in range(chips):
        first = pl.multiple_of((2 * chip_at(place + s, chips, snake) + core) * strip, strip)
        for k, which in enumerate((0, 0, 1, 2)):
            picked[s * strip : (s + 1) * strip, k * 2 * rows : (k + 1) * 2 * rows] = turned[
                pl.ds(which * mid + first, strip), :
            ]
    y = mm(picked[...], stacked[...])
    for s in range(chips):
        y_refs[s][...] = y[s * strip : (s + 1) * strip, :]
    up_ref[...] = y[half * strip : half * strip + strip // 2, :]
    down_ref[...] = y[half * strip + strip // 2 : (half + 1) * strip, :]


def leaf_kernel(chips, snake, *refs):
    half = chips // 2
    device_ref, list_ref, a_refs, f_refs, d_refs = refs[0], refs[1], refs[2:4], refs[4:6], refs[6:8]
    high_ref, low_ref = refs[8:10]
    parts = refs[10 : 10 + 2 * chips]
    keep_refs = refs[10 + 2 * chips : 10 + 3 * chips]
    give_ref, wide, left, right, factors, diags, highs, lows, result, sems, embed_sem = refs[10 + 3 * chips :]
    device = device_ref[0]
    chip, core = device // 2, device % 2
    place = place_of(chip, chips, snake)
    rows, mid = f_refs[0].shape
    leaf = wide.shape[1]
    count = parts[0].shape[0] // TILE
    chip_rows = 2 * rows
    strip = d_refs[0].shape[0]
    copies = []

    for k in range(2):
        fetch(copies, f_refs[k], factors.at[k * rows : (k + 1) * rows, :], sems)
        fetch(copies, d_refs[k], diags.at[k * strip : (k + 1) * strip, :], sems)
    fetch(copies, high_ref, highs, sems)
    fetch(copies, low_ref, lows, sems)
    early = len(copies)
    for step in range(half + 1):
        lane = pl.multiple_of(chip_at(place + step, chips, snake) * chip_rows, chip_rows)
        at = step * chip_rows
        for k in range(2):
            into = left.at[k * rows : (k + 1) * rows, at : at + chip_rows]
            fetch(copies, a_refs[k].at[:, pl.ds(lane, chip_rows)], into, sems)
    wide[...] = jnp.zeros_like(wide)
    for slot in range(chips):
        source = chip_at(place + chips - slot, chips, snake)

        @pl.when(source // half == core)
        def _():
            for side in range(2):
                first = (2 * (source % half) + (core if side == 0 else 1 - core)) * count
                for i in range(count):
                    to = pl.multiple_of(list_ref[core, first + i] * TILE, TILE)
                    block = parts[2 * slot + side].at[i * TILE : (i + 1) * TILE, :]
                    pltpu.make_async_copy(block, wide.at[pl.ds(to, TILE), :], embed_sem).start()

    every = wide.at[: chips * count * TILE, :]
    pltpu.make_async_copy(every, every, embed_sem).wait()
    for step in range(half + 1):
        owner = chip_at(place + step, chips, snake)
        lane = pl.multiple_of(owner * chip_rows, chip_rows)
        at = step * chip_rows
        right[at : at + chip_rows, :] = wide[pl.ds(pl.multiple_of(mid + lane, chip_rows), chip_rows), :]
    at = half * chip_rows
    right[at:, :] = jnp.where(place < half, right[at:, :], jnp.zeros_like(right[at:, :]))
    for copy in copies[:early]:
        copy.wait()
    embed_mid = wide[:mid, :]
    other = 2 * chip + 1 - core
    own = jnp.concatenate(
        [wide[pl.ds(pl.multiple_of(mid + d * rows, rows), rows), :].astype(F32) for d in (device, other)]
    )
    g_high, g_low = split(own - mm(factors[...], embed_mid))
    spread = mm(highs[...], embed_mid) + mm(lows[...], embed_mid)
    i_high, i_low = split(mm(diags[...], embed_mid))
    for copy in copies[early:]:
        copy.wait()
    left[:, :chip_rows] = left[:, :chip_rows] * jnp.bfloat16(0.5)
    s_high, s_low = split(mm(left[...], right[...]) - spread)
    inner = mmt(g_high, s_high) + mmt(g_high, s_low) + mmt(g_low, s_high)
    total = inner + inner.T
    own_mid = jnp.concatenate(
        [wide[pl.ds(pl.multiple_of(d * strip, strip), strip), :] for d in (device, other)]
    )
    result[...] = total + mmt(own_mid, i_high) + mmt(own_mid, i_low)
    band = leaf // chips
    for s in range(chips):
        target = chip_at(place + s, chips, snake)
        mine = target // half == core
        for ref, side in ((keep_refs[s], core), (give_ref.at[s * band : (s + 1) * band, :], 1 - core)):
            value = result[pl.ds(pl.multiple_of((2 * (target % half) + side) * band, band), band), :]
            ref[...] = jnp.where(mine, value, jnp.zeros_like(value))


def solution(mesh):
    parts, devices = mesh.shape["group"], mesh.shape["row"]
    chips = devices // 2
    half = chips // 2
    snake = parts == 2
    order = ring_order(chips, parts)

    def perm(step, keep=lambda source, target, core: True):
        pairs = []
        for p in range(chips):
            target = (p + step) % chips
            for core in range(2):
                if keep(p, target, core):
                    pairs.append((order[p] * 2 + core, order[target] * 2 + core))
        return pairs

    def child_of(p):
        return order[p % chips] // half

    swap_pairs = [(d, d ^ 1) for d in range(devices)]

    def swap(x):
        return lax.ppermute(x, "row", swap_pairs)

    def tie(x, *others):
        return lax.optimization_barrier((x, *others))[0] if others else x

    def ring_start(up, down):
        return lax.ppermute(up, "row", perm(1)), lax.ppermute(down, "row", perm(-1))

    def ring_next(terms, first):
        cut = first[0].shape[0]
        up = terms[half - 1] + jnp.pad(first[0], ((0, cut), (0, 0)))
        down = terms[half + 1] + jnp.pad(first[1], ((cut, 0), (0, 0)))
        return ring_start(up, down)

    def ring_end(terms, second, after):
        up, down = second
        trail = []
        for s in range(half - 2, 0, -1):
            if after and s > 1:
                up, down = tie_pair((up, down), after[len(trail)])
            up, down = ring_start(up + terms[s], down + terms[chips - s])
            trail.append((up, down))
        return terms[0] + up + down, trail

    def tie_pair(pair, others):
        return lax.optimization_barrier((*pair, *others))[:2]

    vmem = pl.BlockSpec(memory_space=pltpu.VMEM)
    smem = pl.BlockSpec(memory_space=pltpu.SMEM)
    anywhere = pl.BlockSpec(memory_space=pl.ANY)
    near_params = pltpu.CompilerParams(vmem_limit_bytes=60 * 2**20)
    mid_params = pltpu.CompilerParams(vmem_limit_bytes=60 * 2**20)
    leaf_params = pltpu.CompilerParams(vmem_limit_bytes=60 * 2**20)

    def near(word, anc_cov, anc_swapped, flows, flow_swaps):
        rows, mid = flows[0].shape
        depth = 2 * rows * half
        return pl.pallas_call(
            lambda *refs: near_kernel(chips, snake, *refs),
            out_shape=jax.ShapeDtypeStruct((2 * rows, mid), F32),
            in_specs=[smem] + [anywhere] * (2 + 2 * half),
            out_specs=vmem,
            scratch_shapes=[
                pltpu.VMEM((2 * rows, depth), BF16),
                pltpu.VMEM((depth, mid), BF16),
                pltpu.SemaphoreType.DMA((6 * half,)),
            ],
            compiler_params=near_params,
            cost_estimate=pl.CostEstimate(flops=7 * 10**9, bytes_accessed=10 * 2**20, transcendentals=0),
            name="near_product",
        )(word, anc_cov, anc_swapped, *[x for pair in zip(flows, flow_swaps) for x in pair])

    def local(anc_cov, mid_factor, mid_diag_inv, leaf_factor, leaf_diag_inv, leaf_rows):
        device = lax.axis_index("row")
        device_word = device.astype(jnp.int32).reshape(1)
        rows, anc = anc_cov.shape
        mid = mid_factor.shape[1]
        leaf = leaf_factor.shape[1]

        leaf_flows, leaf_swaps = [leaf_factor], [swap(leaf_factor)]
        flows, flow_swaps = [mid_factor], [swap(mid_factor)]
        anc_swapped = swap(anc_cov)
        diag_swapped = swap(mid_diag_inv)

        def factor_step(k):
            pairs = perm(-1, (lambda s, t, c: t < half) if k == half else (lambda s, t, c: True))
            deps = [leaf_flows[(3 * (k - 1)) // 2]] + flow_swaps[: k - 1][-1:] if k > 1 else []
            flows.append(lax.ppermute(tie(flows[-1], *deps), "row", pairs))

        def leaf_step(k):
            deps = leaf_swaps[: k - 1][-1:] if k < chips - 1 else []
            if k > 2:
                deps.append(flows[min(half, (5 * (k - 1)) // 8)])
            if k == 2:
                deps.append(diag_swapped)
            if k == 3:
                deps.append(anc_swapped)
            leaf_flows.append(lax.ppermute(tie(leaf_flows[-1], *deps), "row", perm(1)))

        for step in range(1, chips):
            while len(flows) <= half and (3 * (len(flows) - 1)) // 2 < step:
                factor_step(len(flows))
                if len(flows) <= half:
                    flow_swaps.append(swap(flows[-1]))
            if step == chips - 1:
                near_word = tie(device_word, leaf_flows[-2])
                cross = near(near_word, anc_cov, anc_swapped, flows[:half], flow_swaps[:half])
                leaf_flows[-1] = tie(leaf_flows[-1], cross)
            leaf_step(step)
            if step < chips - 1:
                leaf_swaps.append(swap(leaf_flows[-1]))
        flow_swaps.append(swap(tie(flows[-1], leaf_flows[-2])))
        mid_word = tie(device_word, leaf_flows[-2], leaf_swaps[-2])

        strip = mid // devices
        outs = pl.pallas_call(
            lambda *refs: mid_kernel(chips, snake, *refs),
            out_shape=[jax.ShapeDtypeStruct((2 * rows, mid), BF16)] * 2
            + [jax.ShapeDtypeStruct((strip, mid), F32)] * chips
            + [jax.ShapeDtypeStruct((strip // 2, mid), F32)] * 2,
            in_specs=[smem] + [anywhere] * 7,
            out_specs=[vmem] * (4 + chips),
            scratch_shapes=[
                pltpu.VMEM((2 * rows, 2 * rows), BF16),
                pltpu.VMEM((2 * rows, mid), BF16),
                pltpu.VMEM((2 * rows, mid), BF16),
                pltpu.VMEM((2 * rows, mid), F32),
                pltpu.VMEM((3 * mid, 2 * rows), BF16),
                pltpu.VMEM((mid // 2, 8 * rows), BF16),
                pltpu.VMEM((8 * rows, mid), BF16),
                pltpu.SemaphoreType.DMA((9,)),
            ],
            compiler_params=mid_params,
            cost_estimate=pl.CostEstimate(flops=20 * 10**9, bytes_accessed=14 * 2**20, transcendentals=0),
            name="mid_blocks",
        )(mid_word, anc_cov, anc_swapped, flows[0], flow_swaps[0], flows[half], flow_swaps[half], cross)
        c_high, c_low, mid_terms = outs[0], outs[1], outs[2 : 2 + chips]
        mid_first = ring_start(outs[-2], outs[-1])
        leaf_swaps.append(swap(tie(leaf_flows[-1], c_high)))
        leaf_parts = [x for pair in zip(leaf_flows, leaf_swaps) for x in pair]

        band = leaf // chips
        depth = 2 * rows * (half + 1)
        *keep, give = pl.pallas_call(
            lambda *refs: leaf_kernel(chips, snake, *refs),
            out_shape=[jax.ShapeDtypeStruct((band, leaf), F32)] * chips + [jax.ShapeDtypeStruct((leaf, leaf), F32)],
            in_specs=[smem, smem] + [anywhere] * (8 + 2 * chips),
            out_specs=[vmem] * (chips + 1),
            scratch_shapes=[
                pltpu.VMEM((mid + anc, leaf), BF16),
                pltpu.VMEM((2 * rows, depth), BF16),
                pltpu.VMEM((depth, leaf), BF16),
                pltpu.VMEM((2 * rows, mid), BF16),
                pltpu.VMEM((2 * strip, mid), BF16),
                pltpu.VMEM((2 * rows, mid), BF16),
                pltpu.VMEM((2 * rows, mid), BF16),
                pltpu.VMEM((leaf, leaf), F32),
                pltpu.SemaphoreType.DMA((6 + 2 * (half + 1),)),
                pltpu.SemaphoreType.DMA,
            ],
            compiler_params=leaf_params,
            cost_estimate=pl.CostEstimate(flops=2 * 10**10, bytes_accessed=20 * 2**20, transcendentals=0),
            name="leaf_blocks",
        )(
            device_word, leaf_rows, anc_cov, anc_swapped, flows[0], flow_swaps[0], mid_diag_inv, diag_swapped,
            c_high, c_low, *leaf_parts,
        )
        got = swap(tie(give, *mid_first))
        leaf_terms = [keep[s] + got[s * band : (s + 1) * band] for s in range(chips)]
        leaf_far = leaf_terms[half]
        leaf_first = ring_start(leaf_far[: band // 2], leaf_far[band // 2 :])
        mid_second = ring_next(mid_terms, mid_first)
        leaf_second = ring_next(leaf_terms, leaf_first)
        mid_sum, trail = ring_end(mid_terms, mid_second, None)
        leaf_sum, _ = ring_end(leaf_terms, leaf_second, None)
        mid_block = mid_diag_inv.astype(F32) + mid_sum
        leaf_block = leaf_diag_inv.astype(F32) + leaf_sum
        return mid_block, leaf_block

    placed = (
        P(("group", "row"), None),
        P(("group", "row"), None),
        P(("group", "row"), None),
        P(("group", "row"), None),
        P(("group", "row"), None),
        P(),
    )
    return jax.shard_map(
        local,
        mesh=mesh,
        in_specs=placed,
        out_specs=(P(("group", "row"), None), P(("group", "row"), None)),
        check_vma=False,
    )
```

```python
import jax
import jax.numpy as jnp
from jax import lax
from jax.experimental import pallas as pl
from jax.experimental.pallas import tpu as pltpu
from jax.sharding import PartitionSpec as P

TILE = 32
F32 = jnp.float32
BF16 = jnp.bfloat16


def ring_order(chips, parts):
    if parts == 2 and chips % 2 == 0:
        return list(range(0, chips, 2)) + list(range(chips - 1, 0, -2))
    return list(range(chips))


def split(x):
    high = x.astype(BF16)
    return high, (x - high.astype(F32)).astype(BF16)


def mm(a, b):
    return lax.dot_general(a, b, (((1,), (0,)), ((), ())), preferred_element_type=F32)


def mmt(a, b):
    return lax.dot_general(a, b, (((0,), (0,)), ((), ())), preferred_element_type=F32)


def place_of(chip, chips, snake):
    return jnp.where(chip % 2 == 0, chip // 2, chips - 1 - chip // 2) if snake else chip


def chip_at(place, chips, snake):
    place = lax.rem(place, chips)
    return jnp.where(2 * place < chips, 2 * place, 2 * (chips - 1 - place) + 1) if snake else place


def fetch(copies, source, target, sems):
    copies.append(pltpu.make_async_copy(source, target, sems.at[len(copies)]))
    copies[-1].start()


def fetch_columns(copies, a_refs, first, rows, target, at, sems):
    lane = pl.multiple_of(first, rows)
    for k in range(2):
        into = target.at[k * rows : (k + 1) * rows, at : at + rows]
        fetch(copies, a_refs[k].at[:, pl.ds(lane, rows)], into, sems)


def near_kernel(chips, snake, *refs):
    half = chips // 2
    device_ref, a_refs, f_refs = refs[0], refs[1:3], refs[3 : 3 + 2 * half]
    cross_ref, left, right, sems = refs[3 + 2 * half :]
    device = device_ref[0]
    chip, core = device // 2, device % 2
    place = place_of(chip, chips, snake)
    rows = f_refs[0].shape[0]
    copies = []
    for step in range(half):
        owner = chip_at(place + step, chips, snake)
        for side in range(2):
            at = (2 * step + side) * rows
            fetch_columns(copies, a_refs, (2 * owner + (core if side == 0 else 1 - core)) * rows, rows, left, at, sems)
            fetch(copies, f_refs[2 * step + side], right.at[at : at + rows, :], sems)
    for copy in copies[:6]:
        copy.wait()
    left[:, : 2 * rows] = left[:, : 2 * rows] * jnp.bfloat16(0.5)
    cut = 2 * rows * (half // 2)
    for copy in copies[6 : 6 * (half // 2)]:
        copy.wait()
    cross = mm(left[:, :cut], right[:cut, :])
    for copy in copies[6 * (half // 2) :]:
        copy.wait()
    cross_ref[...] = cross + mm(left[:, cut:], right[cut:, :])


def mid_kernel(chips, snake, *refs):
    half = chips // 2
    device_ref, a_refs, own_refs, far_refs, cross_ref = refs[0], refs[1:3], refs[3:5], refs[5:7], refs[7]
    high_ref, low_ref = refs[8:10]
    y_refs = refs[10 : 10 + chips]
    left, right, own, cross, turned, picked, stacked, sems = refs[10 + chips :]
    device = device_ref[0]
    chip, core = device // 2, device % 2
    place = place_of(chip, chips, snake)
    rows, mid = own_refs[0].shape
    copies = []
    fetch(copies, cross_ref, cross, sems)
    for side in range(2):
        fetch(copies, own_refs[side], own.at[side * rows : (side + 1) * rows, :], sems)
    owner = chip_at(place + half, chips, snake)
    for side in range(2):
        lane = (2 * owner + (core if side == 0 else 1 - core)) * rows
        fetch_columns(copies, a_refs, lane, rows, left, side * rows, sems)
        fetch(copies, far_refs[side], right.at[side * rows : (side + 1) * rows, :], sems)
    for copy in copies:
        copy.wait()
    factor = own[...]
    high, low = split(cross[...] + mm(left[...], right[...]))
    high_ref[...] = high
    low_ref[...] = low
    for k, x in enumerate((factor, high, low)):
        turned[k * mid : (k + 1) * mid, :] = x.T
    stacked[: 2 * rows, :] = high
    stacked[2 * rows : 4 * rows, :] = low
    stacked[4 * rows : 6 * rows, :] = factor
    stacked[6 * rows :, :] = factor
    strip = mid // (2 * chips)
    for s in range(chips):
        first = pl.multiple_of((2 * chip_at(place + s, chips, snake) + core) * strip, strip)
        for k, which in enumerate((0, 0, 1, 2)):
            picked[s * strip : (s + 1) * strip, k * 2 * rows : (k + 1) * 2 * rows] = turned[
                pl.ds(which * mid + first, strip), :
            ]
    y = mm(picked[...], stacked[...])
    for s in range(chips):
        y_refs[s][...] = y[s * strip : (s + 1) * strip, :]


def leaf_kernel(chips, snake, *refs):
    half = chips // 2
    device_ref, list_ref, a_refs, f_refs, d_refs = refs[0], refs[1], refs[2:4], refs[4:6], refs[6:8]
    high_ref, low_ref = refs[8:10]
    parts = refs[10 : 10 + 2 * chips]
    keep_refs = refs[10 + 2 * chips : 10 + 3 * chips]
    give_ref, wide, left, right, factors, diags, highs, lows, result, sems, embed_sem = refs[10 + 3 * chips :]
    device = device_ref[0]
    chip, core = device // 2, device % 2
    place = place_of(chip, chips, snake)
    rows, mid = f_refs[0].shape
    leaf = wide.shape[1]
    count = parts[0].shape[0] // TILE
    chip_rows = 2 * rows
    strip = d_refs[0].shape[0]
    copies = []

    for k in range(2):
        fetch(copies, f_refs[k], factors.at[k * rows : (k + 1) * rows, :], sems)
        fetch(copies, d_refs[k], diags.at[k * strip : (k + 1) * strip, :], sems)
    fetch(copies, high_ref, highs, sems)
    fetch(copies, low_ref, lows, sems)
    early = len(copies)
    for step in range(half + 1):
        lane = pl.multiple_of(chip_at(place + step, chips, snake) * chip_rows, chip_rows)
        at = step * chip_rows
        for k in range(2):
            into = left.at[k * rows : (k + 1) * rows, at : at + chip_rows]
            fetch(copies, a_refs[k].at[:, pl.ds(lane, chip_rows)], into, sems)
    wide[...] = jnp.zeros_like(wide)
    for slot in range(chips):
        source = chip_at(place + chips - slot, chips, snake)

        @pl.when(source // half == core)
        def _():
            for side in range(2):
                first = (2 * (source % half) + (core if side == 0 else 1 - core)) * count
                for i in range(count):
                    to = pl.multiple_of(list_ref[core, first + i] * TILE, TILE)
                    block = parts[2 * slot + side].at[i * TILE : (i + 1) * TILE, :]
                    pltpu.make_async_copy(block, wide.at[pl.ds(to, TILE), :], embed_sem).start()

    every = wide.at[: chips * count * TILE, :]
    pltpu.make_async_copy(every, every, embed_sem).wait()
    for step in range(half + 1):
        owner = chip_at(place + step, chips, snake)
        lane = pl.multiple_of(owner * chip_rows, chip_rows)
        at = step * chip_rows
        right[at : at + chip_rows, :] = wide[pl.ds(pl.multiple_of(mid + lane, chip_rows), chip_rows), :]
    at = half * chip_rows
    right[at:, :] = jnp.where(place < half, right[at:, :], jnp.zeros_like(right[at:, :]))
    for copy in copies[:early]:
        copy.wait()
    embed_mid = wide[:mid, :]
    other = 2 * chip + 1 - core
    own = jnp.concatenate(
        [wide[pl.ds(pl.multiple_of(mid + d * rows, rows), rows), :].astype(F32) for d in (device, other)]
    )
    g_high, g_low = split(own - mm(factors[...], embed_mid))
    spread = mm(highs[...], embed_mid) + mm(lows[...], embed_mid)
    i_high, i_low = split(mm(diags[...], embed_mid))
    for copy in copies[early:]:
        copy.wait()
    left[:, :chip_rows] = left[:, :chip_rows] * jnp.bfloat16(0.5)
    s_high, s_low = split(mm(left[...], right[...]) - spread)
    inner = mmt(g_high, s_high) + mmt(g_high, s_low) + mmt(g_low, s_high)
    total = inner + inner.T
    own_mid = jnp.concatenate(
        [wide[pl.ds(pl.multiple_of(d * strip, strip), strip), :] for d in (device, other)]
    )
    result[...] = total + mmt(own_mid, i_high) + mmt(own_mid, i_low)
    band = leaf // chips
    for s in range(chips):
        target = chip_at(place + s, chips, snake)
        mine = target // half == core
        for ref, side in ((keep_refs[s], core), (give_ref.at[s * band : (s + 1) * band, :], 1 - core)):
            value = result[pl.ds(pl.multiple_of((2 * (target % half) + side) * band, band), band), :]
            ref[...] = jnp.where(mine, value, jnp.zeros_like(value))


def solution(mesh):
    parts, devices = mesh.shape["group"], mesh.shape["row"]
    chips = devices // 2
    half = chips // 2
    snake = parts == 2
    order = ring_order(chips, parts)

    def perm(step, keep=lambda source, target, core: True):
        pairs = []
        for p in range(chips):
            target = (p + step) % chips
            for core in range(2):
                if keep(p, target, core):
                    pairs.append((order[p] * 2 + core, order[target] * 2 + core))
        return pairs

    def child_of(p):
        return order[p % chips] // half

    swap_pairs = [(d, d ^ 1) for d in range(devices)]

    def swap(x):
        return lax.ppermute(x, "row", swap_pairs)

    def tie(x, *others):
        return lax.optimization_barrier((x, *others))[0] if others else x

    def send(up, down):
        return lax.ppermute(up, "row", perm(1)), lax.ppermute(down, "row", perm(-1))

    def add_half(term, part, low):
        gap = term.shape[0] - part.shape[0]
        return term + jnp.pad(part, ((0, gap) if low else (gap, 0), (0, 0)))

    def tie_pair(pair, others):
        return lax.optimization_barrier((*pair, *others))[:2]

    vmem = pl.BlockSpec(memory_space=pltpu.VMEM)
    smem = pl.BlockSpec(memory_space=pltpu.SMEM)
    anywhere = pl.BlockSpec(memory_space=pl.ANY)
    near_params = pltpu.CompilerParams(vmem_limit_bytes=60 * 2**20)
    mid_params = pltpu.CompilerParams(vmem_limit_bytes=60 * 2**20)
    leaf_params = pltpu.CompilerParams(vmem_limit_bytes=60 * 2**20)

    def near(word, anc_cov, anc_swapped, flows, flow_swaps):
        rows, mid = flows[0].shape
        depth = 2 * rows * half
        return pl.pallas_call(
            lambda *refs: near_kernel(chips, snake, *refs),
            out_shape=jax.ShapeDtypeStruct((2 * rows, mid), F32),
            in_specs=[smem] + [anywhere] * (2 + 2 * half),
            out_specs=vmem,
            scratch_shapes=[
                pltpu.VMEM((2 * rows, depth), BF16),
                pltpu.VMEM((depth, mid), BF16),
                pltpu.SemaphoreType.DMA((6 * half,)),
            ],
            compiler_params=near_params,
            cost_estimate=pl.CostEstimate(flops=7 * 10**9, bytes_accessed=10 * 2**20, transcendentals=0),
            name="near_product",
        )(word, anc_cov, anc_swapped, *[x for pair in zip(flows, flow_swaps) for x in pair])

    def local(anc_cov, mid_factor, mid_diag_inv, leaf_factor, leaf_diag_inv, leaf_rows):
        device = lax.axis_index("row")
        device_word = device.astype(jnp.int32).reshape(1)
        rows, anc = anc_cov.shape
        mid = mid_factor.shape[1]
        leaf = leaf_factor.shape[1]

        leaf_flows, leaf_swaps = [leaf_factor], [swap(leaf_factor)]
        flows, flow_swaps = [mid_factor], [swap(mid_factor)]
        anc_swapped = swap(anc_cov)
        diag_swapped = swap(mid_diag_inv)

        def factor_step(k):
            pairs = perm(-1, (lambda s, t, c: t < half) if k == half else (lambda s, t, c: True))
            deps = [leaf_flows[(3 * (k - 1)) // 2]] + flow_swaps[: k - 1][-1:] if k > 1 else []
            flows.append(lax.ppermute(tie(flows[-1], *deps), "row", pairs))

        def leaf_step(k):
            deps = leaf_swaps[: k - 1][-1:] if k < chips - 1 else []
            if k > 2:
                deps.append(flows[min(half, (5 * (k - 1)) // 8)])
            if k == 4:
                deps.append(diag_swapped)
            if k == 5:
                deps.append(anc_swapped)
            leaf_flows.append(lax.ppermute(tie(leaf_flows[-1], *deps), "row", perm(1)))

        for step in range(1, chips):
            while len(flows) <= half and (3 * (len(flows) - 1)) // 2 < step:
                factor_step(len(flows))
                if len(flows) <= half:
                    flow_swaps.append(swap(flows[-1]))
            if step == chips - 1:
                near_word = tie(device_word, leaf_flows[-2])
                cross = near(near_word, anc_cov, anc_swapped, flows[:half], flow_swaps[:half])
                leaf_flows[-1] = tie(leaf_flows[-1], cross)
            leaf_step(step)
            if step < chips - 1:
                leaf_swaps.append(swap(leaf_flows[-1]))
        flow_swaps.append(swap(tie(flows[-1], leaf_flows[-2])))
        mid_word = tie(device_word, leaf_flows[-2], leaf_swaps[-2])

        strip = mid // devices
        outs = pl.pallas_call(
            lambda *refs: mid_kernel(chips, snake, *refs),
            out_shape=[jax.ShapeDtypeStruct((2 * rows, mid), BF16)] * 2
            + [jax.ShapeDtypeStruct((strip, mid), F32)] * chips,
            in_specs=[smem] + [anywhere] * 7,
            out_specs=[vmem] * (2 + chips),
            scratch_shapes=[
                pltpu.VMEM((2 * rows, 2 * rows), BF16),
                pltpu.VMEM((2 * rows, mid), BF16),
                pltpu.VMEM((2 * rows, mid), BF16),
                pltpu.VMEM((2 * rows, mid), F32),
                pltpu.VMEM((3 * mid, 2 * rows), BF16),
                pltpu.VMEM((mid // 2, 8 * rows), BF16),
                pltpu.VMEM((8 * rows, mid), BF16),
                pltpu.SemaphoreType.DMA((9,)),
            ],
            compiler_params=mid_params,
            cost_estimate=pl.CostEstimate(flops=20 * 10**9, bytes_accessed=14 * 2**20, transcendentals=0),
            name="mid_blocks",
        )(mid_word, anc_cov, anc_swapped, flows[0], flow_swaps[0], flows[half], flow_swaps[half], cross)
        c_high, c_low, mid_terms = outs[0], outs[1], outs[2:]
        mid_steps = [send(mid_terms[half], mid_terms[half + 1])]
        leaf_swaps.append(swap(tie(leaf_flows[-1], c_high)))
        leaf_parts = [x for pair in zip(leaf_flows, leaf_swaps) for x in pair]

        band = leaf // chips
        depth = 2 * rows * (half + 1)
        *keep, give = pl.pallas_call(
            lambda *refs: leaf_kernel(chips, snake, *refs),
            out_shape=[jax.ShapeDtypeStruct((band, leaf), F32)] * chips + [jax.ShapeDtypeStruct((leaf, leaf), F32)],
            in_specs=[smem, smem] + [anywhere] * (8 + 2 * chips),
            out_specs=[vmem] * (chips + 1),
            scratch_shapes=[
                pltpu.VMEM((mid + anc, leaf), BF16),
                pltpu.VMEM((2 * rows, depth), BF16),
                pltpu.VMEM((depth, leaf), BF16),
                pltpu.VMEM((2 * rows, mid), BF16),
                pltpu.VMEM((2 * strip, mid), BF16),
                pltpu.VMEM((2 * rows, mid), BF16),
                pltpu.VMEM((2 * rows, mid), BF16),
                pltpu.VMEM((leaf, leaf), F32),
                pltpu.SemaphoreType.DMA((6 + 2 * (half + 1),)),
                pltpu.SemaphoreType.DMA,
            ],
            compiler_params=leaf_params,
            cost_estimate=pl.CostEstimate(flops=2 * 10**10, bytes_accessed=20 * 2**20, transcendentals=0),
            name="leaf_blocks",
        )(
            device_word, leaf_rows, anc_cov, anc_swapped, flows[0], flow_swaps[0], mid_diag_inv, diag_swapped,
            c_high, c_low, *leaf_parts,
        )
        got = swap(tie(give, *mid_steps[0]))
        leaf_terms = [keep[s] + got[s * band : (s + 1) * band] for s in range(chips)]
        leaf_far = leaf_terms[half]
        leaf_steps = [send(leaf_far[: band // 2], leaf_far[band // 2 :])]
        for k in range(1, half):
            up, down = mid_steps[-1]
            up = up + mid_terms[half - k]
            if k < half - 1:
                mid_steps.append(send(up, down + mid_terms[half + 1 + k]))
            else:
                mid_steps.append((lax.ppermute(up, "row", perm(1)), down))
            up, down = leaf_steps[-1]
            if k == 1:
                up, down = tie_pair((up, down), mid_steps[-1])
            if k == 1:
                up, down = add_half(leaf_terms[half - 1], up, True), add_half(leaf_terms[half + 1], down, False)
            else:
                up, down = up + leaf_terms[half - k], down + leaf_terms[half + k]
            leaf_steps.append(send(up, down))
        mid_sum = mid_terms[0] + mid_steps[-1][0] + mid_steps[-1][1]
        leaf_sum = leaf_terms[0] + leaf_steps[-1][0] + leaf_steps[-1][1]
        mid_block = mid_diag_inv.astype(F32) + mid_sum
        leaf_block = leaf_diag_inv.astype(F32) + leaf_sum
        return mid_block, leaf_block

    placed = (
        P(("group", "row"), None),
        P(("group", "row"), None),
        P(("group", "row"), None),
        P(("group", "row"), None),
        P(("group", "row"), None),
        P(),
    )
    return jax.shard_map(
        local,
        mesh=mesh,
        in_specs=placed,
        out_specs=(P(("group", "row"), None), P(("group", "row"), None)),
        check_vma=False,
    )
```

```python
import jax
import jax.numpy as jnp
from jax import lax
from jax.experimental import pallas as pl
from jax.experimental.pallas import tpu as pltpu
from jax.sharding import PartitionSpec as P

TILE = 32
F32 = jnp.float32
BF16 = jnp.bfloat16


def ring_order(chips, parts):
    if parts == 2 and chips % 2 == 0:
        return list(range(0, chips, 2)) + list(range(chips - 1, 0, -2))
    return list(range(chips))


def split(x):
    high = x.astype(BF16)
    return high, (x - high.astype(F32)).astype(BF16)


def mm(a, b):
    return lax.dot_general(a, b, (((1,), (0,)), ((), ())), preferred_element_type=F32)


def mmt(a, b):
    return lax.dot_general(a, b, (((0,), (0,)), ((), ())), preferred_element_type=F32)


def place_of(chip, chips, snake):
    return jnp.where(chip % 2 == 0, chip // 2, chips - 1 - chip // 2) if snake else chip


def chip_at(place, chips, snake):
    place = lax.rem(place, chips)
    return jnp.where(2 * place < chips, 2 * place, 2 * (chips - 1 - place) + 1) if snake else place


def fetch(copies, source, target, sems):
    copies.append(pltpu.make_async_copy(source, target, sems.at[len(copies)]))
    copies[-1].start()


def fetch_columns(copies, a_refs, first, rows, target, at, sems):
    lane = pl.multiple_of(first, rows)
    for k in range(2):
        into = target.at[k * rows : (k + 1) * rows, at : at + rows]
        fetch(copies, a_refs[k].at[:, pl.ds(lane, rows)], into, sems)


def near_kernel(chips, snake, *refs):
    half = chips // 2
    device_ref, a_refs, f_refs = refs[0], refs[1:3], refs[3 : 3 + 2 * half]
    cross_ref, left, right, sems = refs[3 + 2 * half :]
    device = device_ref[0]
    chip, core = device // 2, device % 2
    place = place_of(chip, chips, snake)
    rows = f_refs[0].shape[0]
    copies = []
    for step in range(half):
        owner = chip_at(place + step, chips, snake)
        for side in range(2):
            at = (2 * step + side) * rows
            fetch_columns(copies, a_refs, (2 * owner + (core if side == 0 else 1 - core)) * rows, rows, left, at, sems)
            fetch(copies, f_refs[2 * step + side], right.at[at : at + rows, :], sems)
    for copy in copies[:6]:
        copy.wait()
    left[:, : 2 * rows] = left[:, : 2 * rows] * jnp.bfloat16(0.5)
    cut = 2 * rows * (half // 2)
    for copy in copies[6 : 6 * (half // 2)]:
        copy.wait()
    cross = mm(left[:, :cut], right[:cut, :])
    for copy in copies[6 * (half // 2) :]:
        copy.wait()
    cross_ref[...] = cross + mm(left[:, cut:], right[cut:, :])


def mid_kernel(chips, snake, *refs):
    half = chips // 2
    device_ref, a_refs, own_refs, far_refs, cross_ref = refs[0], refs[1:3], refs[3:5], refs[5:7], refs[7]
    high_ref, low_ref = refs[8:10]
    y_refs = refs[10 : 10 + chips]
    left, right, own, cross, turned, picked, stacked, sems = refs[10 + chips :]
    device = device_ref[0]
    chip, core = device // 2, device % 2
    place = place_of(chip, chips, snake)
    rows, mid = own_refs[0].shape
    copies = []
    fetch(copies, cross_ref, cross, sems)
    for side in range(2):
        fetch(copies, own_refs[side], own.at[side * rows : (side + 1) * rows, :], sems)
    owner = chip_at(place + half, chips, snake)
    for side in range(2):
        lane = (2 * owner + (core if side == 0 else 1 - core)) * rows
        fetch_columns(copies, a_refs, lane, rows, left, side * rows, sems)
        fetch(copies, far_refs[side], right.at[side * rows : (side + 1) * rows, :], sems)
    for copy in copies:
        copy.wait()
    factor = own[...]
    high, low = split(cross[...] + mm(left[...], right[...]))
    high_ref[...] = high
    low_ref[...] = low
    for k, x in enumerate((factor, high, low)):
        turned[k * mid : (k + 1) * mid, :] = x.T
    stacked[: 2 * rows, :] = high
    stacked[2 * rows : 4 * rows, :] = low
    stacked[4 * rows : 6 * rows, :] = factor
    stacked[6 * rows :, :] = factor
    strip = mid // (2 * chips)
    for s in range(chips):
        first = pl.multiple_of((2 * chip_at(place + s, chips, snake) + core) * strip, strip)
        for k, which in enumerate((0, 0, 1, 2)):
            picked[s * strip : (s + 1) * strip, k * 2 * rows : (k + 1) * 2 * rows] = turned[
                pl.ds(which * mid + first, strip), :
            ]
    y = mm(picked[...], stacked[...])
    for s in range(chips):
        y_refs[s][...] = y[s * strip : (s + 1) * strip, :]


def leaf_kernel(chips, snake, *refs):
    half = chips // 2
    device_ref, list_ref, a_refs, f_refs, d_refs = refs[0], refs[1], refs[2:4], refs[4:6], refs[6:8]
    high_ref, low_ref = refs[8:10]
    parts = refs[10 : 10 + 2 * chips]
    keep_refs = refs[10 + 2 * chips : 10 + 3 * chips]
    give_ref, wide, left, right, factors, diags, highs, lows, result, sems, embed_sem = refs[10 + 3 * chips :]
    device = device_ref[0]
    chip, core = device // 2, device % 2
    place = place_of(chip, chips, snake)
    rows, mid = f_refs[0].shape
    leaf = wide.shape[1]
    count = parts[0].shape[0] // TILE
    chip_rows = 2 * rows
    strip = d_refs[0].shape[0]
    copies = []

    for k in range(2):
        fetch(copies, f_refs[k], factors.at[k * rows : (k + 1) * rows, :], sems)
        fetch(copies, d_refs[k], diags.at[k * strip : (k + 1) * strip, :], sems)
    fetch(copies, high_ref, highs, sems)
    fetch(copies, low_ref, lows, sems)
    early = len(copies)
    wide[...] = jnp.zeros_like(wide)
    for slot in range(chips):
        source = chip_at(place + chips - slot, chips, snake)

        @pl.when(source // half == core)
        def _():
            for side in range(2):
                first = (2 * (source % half) + (core if side == 0 else 1 - core)) * count
                for i in range(count):
                    to = pl.multiple_of(list_ref[core, first + i] * TILE, TILE)
                    block = parts[2 * slot + side].at[i * TILE : (i + 1) * TILE, :]
                    pltpu.make_async_copy(block, wide.at[pl.ds(to, TILE), :], embed_sem).start()

    for step in range(half + 1):
        lane = pl.multiple_of(chip_at(place + step, chips, snake) * chip_rows, chip_rows)
        at = step * chip_rows
        for k in range(2):
            into = left.at[k * rows : (k + 1) * rows, at : at + chip_rows]
            fetch(copies, a_refs[k].at[:, pl.ds(lane, chip_rows)], into, sems)
    every = wide.at[: chips * count * TILE, :]
    pltpu.make_async_copy(every, every, embed_sem).wait()
    for step in range(half + 1):
        owner = chip_at(place + step, chips, snake)
        lane = pl.multiple_of(owner * chip_rows, chip_rows)
        at = step * chip_rows
        right[at : at + chip_rows, :] = wide[pl.ds(pl.multiple_of(mid + lane, chip_rows), chip_rows), :]
    at = half * chip_rows
    right[at:, :] = jnp.where(place < half, right[at:, :], jnp.zeros_like(right[at:, :]))
    for copy in copies[:early]:
        copy.wait()
    embed_mid = wide[:mid, :]
    other = 2 * chip + 1 - core
    own = jnp.concatenate(
        [wide[pl.ds(pl.multiple_of(mid + d * rows, rows), rows), :].astype(F32) for d in (device, other)]
    )
    g_high, g_low = split(own - mm(factors[...], embed_mid))
    spread = mm(highs[...], embed_mid) + mm(lows[...], embed_mid)
    i_high, i_low = split(mm(diags[...], embed_mid))
    for copy in copies[early:]:
        copy.wait()
    left[:, :chip_rows] = left[:, :chip_rows] * jnp.bfloat16(0.5)
    s_high, s_low = split(mm(left[...], right[...]) - spread)
    inner = mmt(g_high, s_high) + mmt(g_high, s_low) + mmt(g_low, s_high)
    total = inner + inner.T
    own_mid = jnp.concatenate(
        [wide[pl.ds(pl.multiple_of(d * strip, strip), strip), :] for d in (device, other)]
    )
    result[...] = total + mmt(own_mid, i_high) + mmt(own_mid, i_low)
    band = leaf // chips
    for s in range(chips):
        target = chip_at(place + s, chips, snake)
        mine = target // half == core
        for ref, side in ((keep_refs[s], core), (give_ref.at[s * band : (s + 1) * band, :], 1 - core)):
            value = result[pl.ds(pl.multiple_of((2 * (target % half) + side) * band, band), band), :]
            ref[...] = jnp.where(mine, value, jnp.zeros_like(value))


def solution(mesh):
    parts, devices = mesh.shape["group"], mesh.shape["row"]
    chips = devices // 2
    half = chips // 2
    snake = parts == 2
    order = ring_order(chips, parts)

    def perm(step, keep=lambda source, target, core: True):
        pairs = []
        for p in range(chips):
            target = (p + step) % chips
            for core in range(2):
                if keep(p, target, core):
                    pairs.append((order[p] * 2 + core, order[target] * 2 + core))
        return pairs

    def child_of(p):
        return order[p % chips] // half

    swap_pairs = [(d, d ^ 1) for d in range(devices)]

    def swap(x):
        return lax.ppermute(x, "row", swap_pairs)

    def tie(x, *others):
        return lax.optimization_barrier((x, *others))[0] if others else x

    def send(up, down):
        return lax.ppermute(up, "row", perm(1)), lax.ppermute(down, "row", perm(-1))

    def add_half(term, part, low):
        gap = term.shape[0] - part.shape[0]
        return term + jnp.pad(part, ((0, gap) if low else (gap, 0), (0, 0)))

    def tie_pair(pair, others):
        return lax.optimization_barrier((*pair, *others))[:2]

    vmem = pl.BlockSpec(memory_space=pltpu.VMEM)
    smem = pl.BlockSpec(memory_space=pltpu.SMEM)
    anywhere = pl.BlockSpec(memory_space=pl.ANY)
    near_params = pltpu.CompilerParams(vmem_limit_bytes=60 * 2**20)
    mid_params = pltpu.CompilerParams(vmem_limit_bytes=60 * 2**20)
    leaf_params = pltpu.CompilerParams(vmem_limit_bytes=60 * 2**20)

    def near(word, anc_cov, anc_swapped, flows, flow_swaps):
        rows, mid = flows[0].shape
        depth = 2 * rows * half
        return pl.pallas_call(
            lambda *refs: near_kernel(chips, snake, *refs),
            out_shape=jax.ShapeDtypeStruct((2 * rows, mid), F32),
            in_specs=[smem] + [anywhere] * (2 + 2 * half),
            out_specs=vmem,
            scratch_shapes=[
                pltpu.VMEM((2 * rows, depth), BF16),
                pltpu.VMEM((depth, mid), BF16),
                pltpu.SemaphoreType.DMA((6 * half,)),
            ],
            compiler_params=near_params,
            cost_estimate=pl.CostEstimate(flops=7 * 10**9, bytes_accessed=10 * 2**20, transcendentals=0),
            name="near_product",
        )(word, anc_cov, anc_swapped, *[x for pair in zip(flows, flow_swaps) for x in pair])

    def local(anc_cov, mid_factor, mid_diag_inv, leaf_factor, leaf_diag_inv, leaf_rows):
        device = lax.axis_index("row")
        device_word = device.astype(jnp.int32).reshape(1)
        rows, anc = anc_cov.shape
        mid = mid_factor.shape[1]
        leaf = leaf_factor.shape[1]

        leaf_flows, leaf_swaps = [leaf_factor], [swap(leaf_factor)]
        flows, flow_swaps = [mid_factor], [swap(mid_factor)]
        anc_swapped = swap(anc_cov)
        diag_swapped = swap(mid_diag_inv)

        def factor_step(k):
            pairs = perm(-1, (lambda s, t, c: t < half) if k == half else (lambda s, t, c: True))
            deps = [leaf_flows[(3 * (k - 1)) // 2]] + flow_swaps[: k - 1][-1:] if k > 1 else []
            flows.append(lax.ppermute(tie(flows[-1], *deps), "row", pairs))

        def leaf_step(k):
            deps = leaf_swaps[: k - 1][-1:] if k < chips - 1 else []
            if k > 2:
                deps.append(flows[min(half, (5 * (k - 1)) // 8)])
            if k == 4:
                deps.append(diag_swapped)
            if k == 5:
                deps.append(anc_swapped)
            leaf_flows.append(lax.ppermute(tie(leaf_flows[-1], *deps), "row", perm(1)))

        for step in range(1, chips):
            while len(flows) <= half and (3 * (len(flows) - 1)) // 2 < step:
                factor_step(len(flows))
                if len(flows) <= half:
                    flow_swaps.append(swap(flows[-1]))
            if step == chips - 1:
                near_word = tie(device_word, leaf_flows[-2])
                cross = near(near_word, anc_cov, anc_swapped, flows[:half], flow_swaps[:half])
                leaf_flows[-1] = tie(leaf_flows[-1], cross)
            leaf_step(step)
            if step < chips - 1:
                leaf_swaps.append(swap(leaf_flows[-1]))
        flow_swaps.append(swap(tie(flows[-1], leaf_flows[-2])))
        mid_word = tie(device_word, leaf_flows[-2])

        strip = mid // devices
        outs = pl.pallas_call(
            lambda *refs: mid_kernel(chips, snake, *refs),
            out_shape=[jax.ShapeDtypeStruct((2 * rows, mid), BF16)] * 2
            + [jax.ShapeDtypeStruct((strip, mid), F32)] * chips,
            in_specs=[smem] + [anywhere] * 7,
            out_specs=[vmem] * (2 + chips),
            scratch_shapes=[
                pltpu.VMEM((2 * rows, 2 * rows), BF16),
                pltpu.VMEM((2 * rows, mid), BF16),
                pltpu.VMEM((2 * rows, mid), BF16),
                pltpu.VMEM((2 * rows, mid), F32),
                pltpu.VMEM((3 * mid, 2 * rows), BF16),
                pltpu.VMEM((mid // 2, 8 * rows), BF16),
                pltpu.VMEM((8 * rows, mid), BF16),
                pltpu.SemaphoreType.DMA((9,)),
            ],
            compiler_params=mid_params,
            cost_estimate=pl.CostEstimate(flops=20 * 10**9, bytes_accessed=14 * 2**20, transcendentals=0),
            name="mid_blocks",
        )(mid_word, anc_cov, anc_swapped, flows[0], flow_swaps[0], flows[half], flow_swaps[half], cross)
        c_high, c_low, mid_terms = outs[0], outs[1], outs[2:]
        mid_steps = [send(mid_terms[half], mid_terms[half + 1])]
        leaf_swaps.append(swap(tie(leaf_flows[-1], c_high)))
        leaf_parts = [x for pair in zip(leaf_flows, leaf_swaps) for x in pair]

        band = leaf // chips
        depth = 2 * rows * (half + 1)
        *keep, give = pl.pallas_call(
            lambda *refs: leaf_kernel(chips, snake, *refs),
            out_shape=[jax.ShapeDtypeStruct((band, leaf), F32)] * chips + [jax.ShapeDtypeStruct((leaf, leaf), F32)],
            in_specs=[smem, smem] + [anywhere] * (8 + 2 * chips),
            out_specs=[vmem] * (chips + 1),
            scratch_shapes=[
                pltpu.VMEM((mid + anc, leaf), BF16),
                pltpu.VMEM((2 * rows, depth), BF16),
                pltpu.VMEM((depth, leaf), BF16),
                pltpu.VMEM((2 * rows, mid), BF16),
                pltpu.VMEM((2 * strip, mid), BF16),
                pltpu.VMEM((2 * rows, mid), BF16),
                pltpu.VMEM((2 * rows, mid), BF16),
                pltpu.VMEM((leaf, leaf), F32),
                pltpu.SemaphoreType.DMA((6 + 2 * (half + 1),)),
                pltpu.SemaphoreType.DMA,
            ],
            compiler_params=leaf_params,
            cost_estimate=pl.CostEstimate(flops=2 * 10**10, bytes_accessed=20 * 2**20, transcendentals=0),
            name="leaf_blocks",
        )(
            device_word, leaf_rows, anc_cov, anc_swapped, flows[0], flow_swaps[0], mid_diag_inv, diag_swapped,
            c_high, c_low, *leaf_parts,
        )
        got = swap(tie(give, *mid_steps[0]))
        leaf_terms = [keep[s] + got[s * band : (s + 1) * band] for s in range(chips)]
        leaf_far = leaf_terms[half]
        leaf_steps = [send(leaf_far[: band // 2], leaf_far[band // 2 :])]
        for k in range(1, half):
            up, down = mid_steps[-1]
            up = up + mid_terms[half - k]
            if k < half - 1:
                mid_steps.append(send(up, down + mid_terms[half + 1 + k]))
            else:
                mid_steps.append((lax.ppermute(up, "row", perm(1)), down))
            up, down = leaf_steps[-1]
            if k == 1:
                up, down = tie_pair((up, down), mid_steps[-1])
            if k == 1:
                up, down = add_half(leaf_terms[half - 1], up, True), add_half(leaf_terms[half + 1], down, False)
            else:
                up, down = up + leaf_terms[half - k], down + leaf_terms[half + k]
            leaf_steps.append(send(up, down))
        mid_sum = mid_terms[0] + mid_steps[-1][0] + mid_steps[-1][1]
        leaf_sum = leaf_terms[0] + leaf_steps[-1][0] + leaf_steps[-1][1]
        mid_block = mid_diag_inv.astype(F32) + mid_sum
        leaf_block = leaf_diag_inv.astype(F32) + leaf_sum
        return mid_block, leaf_block

    placed = (
        P(("group", "row"), None),
        P(("group", "row"), None),
        P(("group", "row"), None),
        P(("group", "row"), None),
        P(("group", "row"), None),
        P(),
    )
    return jax.shard_map(
        local,
        mesh=mesh,
        in_specs=placed,
        out_specs=(P(("group", "row"), None), P(("group", "row"), None)),
        check_vma=False,
    )
```

```python
import jax
import jax.numpy as jnp
from jax import lax
from jax.experimental import pallas as pl
from jax.experimental.pallas import tpu as pltpu
from jax.sharding import PartitionSpec as P

TILE = 32
F32 = jnp.float32
BF16 = jnp.bfloat16


def ring_order(chips, parts):
    if parts == 2 and chips % 2 == 0:
        return list(range(0, chips, 2)) + list(range(chips - 1, 0, -2))
    return list(range(chips))


def split(x):
    high = x.astype(BF16)
    return high, (x - high.astype(F32)).astype(BF16)


def mm(a, b):
    return lax.dot_general(a, b, (((1,), (0,)), ((), ())), preferred_element_type=F32)


def mmt(a, b):
    return lax.dot_general(a, b, (((0,), (0,)), ((), ())), preferred_element_type=F32)


def place_of(chip, chips, snake):
    return jnp.where(chip % 2 == 0, chip // 2, chips - 1 - chip // 2) if snake else chip


def chip_at(place, chips, snake):
    place = lax.rem(place, chips)
    return jnp.where(2 * place < chips, 2 * place, 2 * (chips - 1 - place) + 1) if snake else place


def fetch(copies, source, target, sems):
    copies.append(pltpu.make_async_copy(source, target, sems.at[len(copies)]))
    copies[-1].start()


def fetch_columns(copies, a_refs, first, rows, target, at, sems):
    lane = pl.multiple_of(first, rows)
    for k in range(2):
        into = target.at[k * rows : (k + 1) * rows, at : at + rows]
        fetch(copies, a_refs[k].at[:, pl.ds(lane, rows)], into, sems)


def near_kernel(chips, snake, *refs):
    half = chips // 2
    device_ref, a_refs, f_refs = refs[0], refs[1:3], refs[3 : 3 + 2 * half]
    cross_ref, left, right, sems = refs[3 + 2 * half :]
    device = device_ref[0]
    chip, core = device // 2, device % 2
    place = place_of(chip, chips, snake)
    rows = f_refs[0].shape[0]
    copies = []
    for step in range(half):
        owner = chip_at(place + step, chips, snake)
        for side in range(2):
            at = (2 * step + side) * rows
            fetch_columns(copies, a_refs, (2 * owner + (core if side == 0 else 1 - core)) * rows, rows, left, at, sems)
            fetch(copies, f_refs[2 * step + side], right.at[at : at + rows, :], sems)
    for copy in copies[:6]:
        copy.wait()
    left[:, : 2 * rows] = left[:, : 2 * rows] * jnp.bfloat16(0.5)
    cut = 2 * rows * (half // 2)
    for copy in copies[6 : 6 * (half // 2)]:
        copy.wait()
    cross = mm(left[:, :cut], right[:cut, :])
    for copy in copies[6 * (half // 2) :]:
        copy.wait()
    cross_ref[...] = cross + mm(left[:, cut:], right[cut:, :])


def mid_kernel(chips, snake, *refs):
    half = chips // 2
    device_ref, a_refs, own_refs, far_refs, cross_ref = refs[0], refs[1:3], refs[3:5], refs[5:7], refs[7]
    high_ref, low_ref = refs[8:10]
    y_refs = refs[10 : 10 + chips]
    left, right, own, cross, turned, picked, stacked, sems = refs[10 + chips :]
    device = device_ref[0]
    chip, core = device // 2, device % 2
    place = place_of(chip, chips, snake)
    rows, mid = own_refs[0].shape
    copies = []
    for side in range(2):
        fetch(copies, own_refs[side], own.at[side * rows : (side + 1) * rows, :], sems)
    owner = chip_at(place + half, chips, snake)
    for side in range(2):
        lane = (2 * owner + (core if side == 0 else 1 - core)) * rows
        fetch_columns(copies, a_refs, lane, rows, left, side * rows, sems)
        fetch(copies, far_refs[side], right.at[side * rows : (side + 1) * rows, :], sems)
    fetch(copies, cross_ref, cross, sems)
    for copy in copies[:-1]:
        copy.wait()
    far = mm(left[...], right[...])
    copies[-1].wait()
    factor = own[...]
    high, low = split(cross[...] + far)
    high_ref[...] = high
    low_ref[...] = low
    for k, x in enumerate((factor, high, low)):
        turned[k * mid : (k + 1) * mid, :] = x.T
    stacked[: 2 * rows, :] = high
    stacked[2 * rows : 4 * rows, :] = low
    stacked[4 * rows : 6 * rows, :] = factor
    stacked[6 * rows :, :] = factor
    strip = mid // (2 * chips)
    for s in range(chips):
        first = pl.multiple_of((2 * chip_at(place + s, chips, snake) + core) * strip, strip)
        for k, which in enumerate((0, 0, 1, 2)):
            picked[s * strip : (s + 1) * strip, k * 2 * rows : (k + 1) * 2 * rows] = turned[
                pl.ds(which * mid + first, strip), :
            ]
    y = mm(picked[...], stacked[...])
    for s in range(chips):
        y_refs[s][...] = y[s * strip : (s + 1) * strip, :]


def leaf_kernel(chips, snake, *refs):
    half = chips // 2
    device_ref, list_ref, a_refs, f_refs, d_refs = refs[0], refs[1], refs[2:4], refs[4:6], refs[6:8]
    high_ref, low_ref = refs[8:10]
    parts = refs[10 : 10 + 2 * chips]
    keep_refs = refs[10 + 2 * chips : 10 + 3 * chips]
    give_ref, wide, left, right, factors, diags, highs, lows, result, sems, embed_sem = refs[10 + 3 * chips :]
    device = device_ref[0]
    chip, core = device // 2, device % 2
    place = place_of(chip, chips, snake)
    rows, mid = f_refs[0].shape
    leaf = wide.shape[1]
    count = parts[0].shape[0] // TILE
    chip_rows = 2 * rows
    strip = d_refs[0].shape[0]
    copies = []

    for k in range(2):
        fetch(copies, f_refs[k], factors.at[k * rows : (k + 1) * rows, :], sems)
        fetch(copies, d_refs[k], diags.at[k * strip : (k + 1) * strip, :], sems)
    fetch(copies, high_ref, highs, sems)
    fetch(copies, low_ref, lows, sems)
    early = len(copies)
    wide[...] = jnp.zeros_like(wide)
    for slot in range(chips):
        source = chip_at(place + chips - slot, chips, snake)

        @pl.when(source // half == core)
        def _():
            for side in range(2):
                first = (2 * (source % half) + (core if side == 0 else 1 - core)) * count
                for i in range(count):
                    to = pl.multiple_of(list_ref[core, first + i] * TILE, TILE)
                    block = parts[2 * slot + side].at[i * TILE : (i + 1) * TILE, :]
                    pltpu.make_async_copy(block, wide.at[pl.ds(to, TILE), :], embed_sem).start()

    for step in range(half + 1):
        lane = pl.multiple_of(chip_at(place + step, chips, snake) * chip_rows, chip_rows)
        at = step * chip_rows
        for k in range(2):
            into = left.at[k * rows : (k + 1) * rows, at : at + chip_rows]
            fetch(copies, a_refs[k].at[:, pl.ds(lane, chip_rows)], into, sems)
    every = wide.at[: chips * count * TILE, :]
    pltpu.make_async_copy(every, every, embed_sem).wait()
    for step in range(half + 1):
        owner = chip_at(place + step, chips, snake)
        lane = pl.multiple_of(owner * chip_rows, chip_rows)
        at = step * chip_rows
        right[at : at + chip_rows, :] = wide[pl.ds(pl.multiple_of(mid + lane, chip_rows), chip_rows), :]
    at = half * chip_rows
    right[at:, :] = jnp.where(place < half, right[at:, :], jnp.zeros_like(right[at:, :]))
    for copy in copies[:early]:
        copy.wait()
    embed_mid = wide[:mid, :]
    other = 2 * chip + 1 - core
    own = jnp.concatenate(
        [wide[pl.ds(pl.multiple_of(mid + d * rows, rows), rows), :].astype(F32) for d in (device, other)]
    )
    g_high, g_low = split(own - mm(factors[...], embed_mid))
    spread = mm(highs[...], embed_mid) + mm(lows[...], embed_mid)
    i_high, i_low = split(mm(diags[...], embed_mid))
    for copy in copies[early:]:
        copy.wait()
    left[:, :chip_rows] = left[:, :chip_rows] * jnp.bfloat16(0.5)
    s_high, s_low = split(mm(left[...], right[...]) - spread)
    inner = mmt(g_high, s_high) + mmt(g_high, s_low) + mmt(g_low, s_high)
    total = inner + inner.T
    own_mid = jnp.concatenate(
        [wide[pl.ds(pl.multiple_of(d * strip, strip), strip), :] for d in (device, other)]
    )
    result[...] = total + mmt(own_mid, i_high) + mmt(own_mid, i_low)
    band = leaf // chips
    for s in range(chips):
        target = chip_at(place + s, chips, snake)
        mine = target // half == core
        for ref, side in ((keep_refs[s], core), (give_ref.at[s * band : (s + 1) * band, :], 1 - core)):
            value = result[pl.ds(pl.multiple_of((2 * (target % half) + side) * band, band), band), :]
            ref[...] = jnp.where(mine, value, jnp.zeros_like(value))


def solution(mesh):
    parts, devices = mesh.shape["group"], mesh.shape["row"]
    chips = devices // 2
    half = chips // 2
    snake = parts == 2
    order = ring_order(chips, parts)

    def perm(step, keep=lambda source, target, core: True):
        pairs = []
        for p in range(chips):
            target = (p + step) % chips
            for core in range(2):
                if keep(p, target, core):
                    pairs.append((order[p] * 2 + core, order[target] * 2 + core))
        return pairs

    def child_of(p):
        return order[p % chips] // half

    swap_pairs = [(d, d ^ 1) for d in range(devices)]

    def swap(x):
        return lax.ppermute(x, "row", swap_pairs)

    def tie(x, *others):
        return lax.optimization_barrier((x, *others))[0] if others else x

    def send(up, down):
        return lax.ppermute(up, "row", perm(1)), lax.ppermute(down, "row", perm(-1))

    def add_half(term, part, low):
        gap = term.shape[0] - part.shape[0]
        return term + jnp.pad(part, ((0, gap) if low else (gap, 0), (0, 0)))

    def tie_pair(pair, others):
        return lax.optimization_barrier((*pair, *others))[:2]

    vmem = pl.BlockSpec(memory_space=pltpu.VMEM)
    smem = pl.BlockSpec(memory_space=pltpu.SMEM)
    anywhere = pl.BlockSpec(memory_space=pl.ANY)
    near_params = pltpu.CompilerParams(vmem_limit_bytes=60 * 2**20)
    mid_params = pltpu.CompilerParams(vmem_limit_bytes=60 * 2**20)
    leaf_params = pltpu.CompilerParams(vmem_limit_bytes=60 * 2**20)

    def near(word, anc_cov, anc_swapped, flows, flow_swaps):
        rows, mid = flows[0].shape
        depth = 2 * rows * half
        return pl.pallas_call(
            lambda *refs: near_kernel(chips, snake, *refs),
            out_shape=jax.ShapeDtypeStruct((2 * rows, mid), F32),
            in_specs=[smem] + [anywhere] * (2 + 2 * half),
            out_specs=vmem,
            scratch_shapes=[
                pltpu.VMEM((2 * rows, depth), BF16),
                pltpu.VMEM((depth, mid), BF16),
                pltpu.SemaphoreType.DMA((6 * half,)),
            ],
            compiler_params=near_params,
            cost_estimate=pl.CostEstimate(flops=7 * 10**9, bytes_accessed=10 * 2**20, transcendentals=0),
            name="near_product",
        )(word, anc_cov, anc_swapped, *[x for pair in zip(flows, flow_swaps) for x in pair])

    def local(anc_cov, mid_factor, mid_diag_inv, leaf_factor, leaf_diag_inv, leaf_rows):
        device = lax.axis_index("row")
        device_word = device.astype(jnp.int32).reshape(1)
        rows, anc = anc_cov.shape
        mid = mid_factor.shape[1]
        leaf = leaf_factor.shape[1]

        leaf_flows, leaf_swaps = [leaf_factor], [swap(leaf_factor)]
        flows, flow_swaps = [mid_factor], [swap(mid_factor)]
        anc_swapped = swap(anc_cov)
        diag_swapped = swap(mid_diag_inv)

        def factor_step(k):
            pairs = perm(-1, (lambda s, t, c: t < half) if k == half else (lambda s, t, c: True))
            deps = [leaf_flows[(3 * (k - 1)) // 2]] + flow_swaps[: k - 1][-1:] if k > 1 else []
            flows.append(lax.ppermute(tie(flows[-1], *deps), "row", pairs))

        def leaf_step(k):
            deps = leaf_swaps[: k - 1][-1:] if k < chips - 1 else []
            if k > 2:
                deps.append(flows[min(half, (5 * (k - 1)) // 8)])
            if k == 4:
                deps.append(diag_swapped)
            if k == 5:
                deps.append(anc_swapped)
            leaf_flows.append(lax.ppermute(tie(leaf_flows[-1], *deps), "row", perm(1)))

        for step in range(1, chips):
            while len(flows) <= half and (3 * (len(flows) - 1)) // 2 < step:
                factor_step(len(flows))
                if len(flows) <= half:
                    flow_swaps.append(swap(flows[-1]))
            if step == chips - 1:
                near_word = tie(device_word, leaf_flows[-2])
                cross = near(near_word, anc_cov, anc_swapped, flows[:half], flow_swaps[:half])
                leaf_flows[-1] = tie(leaf_flows[-1], cross)
            leaf_step(step)
            if step < chips - 1:
                leaf_swaps.append(swap(leaf_flows[-1]))
        flow_swaps.append(swap(tie(flows[-1], leaf_flows[-2])))
        mid_word = tie(device_word, leaf_flows[-2])

        strip = mid // devices
        outs = pl.pallas_call(
            lambda *refs: mid_kernel(chips, snake, *refs),
            out_shape=[jax.ShapeDtypeStruct((2 * rows, mid), BF16)] * 2
            + [jax.ShapeDtypeStruct((strip, mid), F32)] * chips,
            in_specs=[smem] + [anywhere] * 7,
            out_specs=[vmem] * (2 + chips),
            scratch_shapes=[
                pltpu.VMEM((2 * rows, 2 * rows), BF16),
                pltpu.VMEM((2 * rows, mid), BF16),
                pltpu.VMEM((2 * rows, mid), BF16),
                pltpu.VMEM((2 * rows, mid), F32),
                pltpu.VMEM((3 * mid, 2 * rows), BF16),
                pltpu.VMEM((mid // 2, 8 * rows), BF16),
                pltpu.VMEM((8 * rows, mid), BF16),
                pltpu.SemaphoreType.DMA((9,)),
            ],
            compiler_params=mid_params,
            cost_estimate=pl.CostEstimate(flops=20 * 10**9, bytes_accessed=14 * 2**20, transcendentals=0),
            name="mid_blocks",
        )(mid_word, anc_cov, anc_swapped, flows[0], flow_swaps[0], flows[half], flow_swaps[half], cross)
        c_high, c_low, mid_terms = outs[0], outs[1], outs[2:]
        mid_steps = [send(mid_terms[half], mid_terms[half + 1])]
        leaf_swaps.append(swap(tie(leaf_flows[-1], c_high)))
        leaf_parts = [x for pair in zip(leaf_flows, leaf_swaps) for x in pair]

        band = leaf // chips
        depth = 2 * rows * (half + 1)
        *keep, give = pl.pallas_call(
            lambda *refs: leaf_kernel(chips, snake, *refs),
            out_shape=[jax.ShapeDtypeStruct((band, leaf), F32)] * chips + [jax.ShapeDtypeStruct((leaf, leaf), F32)],
            in_specs=[smem, smem] + [anywhere] * (8 + 2 * chips),
            out_specs=[vmem] * (chips + 1),
            scratch_shapes=[
                pltpu.VMEM((mid + anc, leaf), BF16),
                pltpu.VMEM((2 * rows, depth), BF16),
                pltpu.VMEM((depth, leaf), BF16),
                pltpu.VMEM((2 * rows, mid), BF16),
                pltpu.VMEM((2 * strip, mid), BF16),
                pltpu.VMEM((2 * rows, mid), BF16),
                pltpu.VMEM((2 * rows, mid), BF16),
                pltpu.VMEM((leaf, leaf), F32),
                pltpu.SemaphoreType.DMA((6 + 2 * (half + 1),)),
                pltpu.SemaphoreType.DMA,
            ],
            compiler_params=leaf_params,
            cost_estimate=pl.CostEstimate(flops=2 * 10**10, bytes_accessed=20 * 2**20, transcendentals=0),
            name="leaf_blocks",
        )(
            device_word, leaf_rows, anc_cov, anc_swapped, flows[0], flow_swaps[0], mid_diag_inv, diag_swapped,
            c_high, c_low, *leaf_parts,
        )
        got = swap(tie(give, *mid_steps[0]))
        leaf_terms = [keep[s] + got[s * band : (s + 1) * band] for s in range(chips)]
        leaf_far = leaf_terms[half]
        leaf_steps = [send(leaf_far[: band // 2], leaf_far[band // 2 :])]
        for k in range(1, half):
            up, down = mid_steps[-1]
            up = up + mid_terms[half - k]
            if k < half - 1:
                mid_steps.append(send(up, down + mid_terms[half + 1 + k]))
            else:
                mid_steps.append((lax.ppermute(up, "row", perm(1)), down))
            up, down = leaf_steps[-1]
            if k == 1:
                up, down = tie_pair((up, down), mid_steps[-1])
            if k == 1:
                up, down = add_half(leaf_terms[half - 1], up, True), add_half(leaf_terms[half + 1], down, False)
            else:
                up, down = up + leaf_terms[half - k], down + leaf_terms[half + k]
            leaf_steps.append(send(up, down))
        mid_sum = mid_terms[0] + mid_steps[-1][0] + mid_steps[-1][1]
        leaf_sum = leaf_terms[0] + leaf_steps[-1][0] + leaf_steps[-1][1]
        mid_block = mid_diag_inv.astype(F32) + mid_sum
        leaf_block = leaf_diag_inv.astype(F32) + leaf_sum
        return mid_block, leaf_block

    placed = (
        P(("group", "row"), None),
        P(("group", "row"), None),
        P(("group", "row"), None),
        P(("group", "row"), None),
        P(("group", "row"), None),
        P(),
    )
    return jax.shard_map(
        local,
        mesh=mesh,
        in_specs=placed,
        out_specs=(P(("group", "row"), None), P(("group", "row"), None)),
        check_vma=False,
    )
```
